256 devices in a mesh: con: 8 (over x, core), tile: 32 (over y, z).
Axes of the slice: x: 4, y: 4, z: 8, core: 2. Of those that a mesh axis runs over, the one named last changes fastest.
Arguments:
- first_guess: float32 [8, 2, 512, 2048], P('con', None, 'tile'), may hold values from -4 to 4
- misfit: float32 [8, 2, 512, 2048], P('con', None, 'tile'), may hold values from -6 to 6
- innovations: float32 [8, 2, 8192], P('con', None, 'tile'), may hold values from -6 to 6
- obs_cells: int32 [8192], P('tile'), may hold values from 0 to 32767
- depth: float32 [512, 2048], P('tile'), may hold values from 1 to 8
- base_speed: float32 [512, 2048], P('tile'), may hold values from 0.1 to 1
- frequency: float32 [8], P('con'), may hold values from 0.5 to 3
Outputs:
- adjoint: float32 [8, 2, 512, 2048], P('con', None, 'tile')
The draws below stay inside these ranges and needn't reach their ends.
Inputs may be any that keep to these rules, and one draw needn't show every extreme that they name: `obs_cells`: an observation's cell lies in the tile that holds it; several observations may share a cell.
All inputs are finite; a program needn't handle non-finite values.
Results may differ from the reference program's by a relative error of at most 0.00002.
Values sent between devices are 32-bit elements; how exact they have to be, the bound alone decides.
No kernel may reach another device: no remote copies, remote signals or barrier semaphores. Data moves between devices by JAX's collectives and lax.ppermute only.
A program may use at most 64 MiB of HBM per device.

```python
import math
import jax
import jax.numpy as jnp

TILE_ROWS = 16
LANES = 2048
OBS_DEV = 256
SWEEPS = 16
NCON = 8
NROWS = 512
NOBS = 8192


def place_ends(values, rng, smallest, high):
    longest = values.shape.index(max(values.shape))
    spots = []
    for shift in (0, 1):
        where = [jax.random.randint(jax.random.fold_in(rng, axis), (), 0, length) for axis, length in enumerate(values.shape)]
        where[longest] = (where[longest] + shift) % values.shape[longest]
        spots.append(tuple(where))
    return values.at[spots[0]].set(smallest).at[spots[1]].set(high)


def block_scale(own_key, dims, split, low, largest):
    gain, own = 1.0, jax.random.fold_in(own_key, 6)
    for dim, blocks in split:
        draws = jnp.exp(jax.random.uniform(jax.random.fold_in(own, dim), (blocks,), jnp.float32, low / len(split), largest / len(split)))
        gain = gain * jnp.repeat(draws, dims[dim] // blocks).reshape([-1 if axis == dim else 1 for axis in range(len(dims))])
    return gain


def centred(rng, dims, spread, limit, pieces=(), held_as=jnp.bfloat16):
    factor_of = block_scale(rng, dims, pieces, -0.22, 0.18) if pieces else 1.0
    drawn = jax.random.normal(rng, dims, jnp.float32) * spread * factor_of
    return jnp.minimum(jnp.maximum(drawn, -limit), limit).astype(held_as)


def setup_inputs(seed: int = 0) -> dict:
    key_list = jax.random.split(jax.random.key(seed), 8)
    return {
        "first_guess": centred(key_list[0], (NCON, 2, NROWS, LANES), 0.5, 4.0, ((0, 8), (2, 32)), jnp.float32),
        "misfit": centred(key_list[1], (NCON, 2, NROWS, LANES), 1.0, 6.0, ((0, 8), (2, 32)), jnp.float32),
        "innovations": centred(key_list[2], (NCON, 2, NOBS), 1.0, 6.0, ((0, 8), (2, 32)), jnp.float32),
        "obs_cells": place_ends(jax.random.randint(key_list[3], (NOBS,), 0, TILE_ROWS * LANES), jax.random.fold_in(key_list[3], 1), 0, (TILE_ROWS * LANES) - 1).astype(jnp.int32),
        "depth": jnp.clip(jnp.exp(math.log(8.0) - 2.0794415 * jax.random.uniform(key_list[4], (NROWS, LANES), jnp.float32) ** block_scale(key_list[4], (NROWS, LANES), ((0, 32),), -0.2, 0.2)), 1.0, 8.0),
        "base_speed": jnp.clip(jnp.exp(math.log(1.0) - 2.3025851 * jax.random.uniform(key_list[5], (NROWS, LANES), jnp.float32) ** block_scale(key_list[5], (NROWS, LANES), ((0, 32),), -0.2, 0.2)), 0.1, 1.0),
        "frequency": jnp.clip(jnp.exp(math.log(3.0) - 1.7917595 * jax.random.uniform(key_list[6], (NCON,), jnp.float32) ** block_scale(key_list[6], (NCON,), ((0, 8),), -0.2, 0.2)), 0.5, 3.0),
    }


DRAG_COEF = 0.5
SHIFT_SIGMA = 0.1

def coefficients(speed_sq, depth_cells, angular):
    drag = DRAG_COEF * jnp.sqrt(speed_sq)
    modulus = drag * drag + angular * angular
    gain_real = depth_cells * drag / modulus
    gain_imag = depth_cells * angular / modulus
    diag_real = SHIFT_SIGMA + 4.0 * gain_real
    diag_imag = angular + 4.0 * gain_imag
    norm_sq = diag_real * diag_real + diag_imag * diag_imag
    return (gain_real, gain_imag, diag_real / norm_sq, -diag_imag / norm_sq)

def neighbours(extended):
    middle = extended[:, 1:-1]
    along = extended[:, 2:] + extended[:, :-2]
    padded = jnp.pad(middle, ((0, 0), (0, 0), (1, 1)))
    across = padded[:, :, 2:] + padded[:, :, :-2]
    return along + across

def relax(neighbour_sum, forcing, coefficient):
    gain_real, gain_imag, inv_real, inv_imag = coefficient
    numer_real = forcing[0] + gain_real * neighbour_sum[0] - gain_imag * neighbour_sum[1]
    numer_imag = forcing[1] + gain_real * neighbour_sum[1] + gain_imag * neighbour_sum[0]
    return jnp.stack([numer_real * inv_real - numer_imag * inv_imag, numer_real * inv_imag + numer_imag * inv_real])

def squared(field):
    return field[0] * field[0] + field[1] * field[1]

def reference(first_guess, misfit, innovations, obs_cells, depth, base_speed, frequency):
    shape = first_guess.shape
    lane_count = shape[3]
    tile_of = (jnp.arange(obs_cells.shape[0]) // OBS_DEV).astype(jnp.int32)
    flat_cells = tile_of * (TILE_ROWS * lane_count) + obs_cells
    forcing = misfit.reshape(shape[0], 2, -1).at[:, :, flat_cells].add(innovations).reshape(shape)
    adjoints = [first_guess[other] for other in range(shape[0])]
    squares = [squared(field) for field in adjoints]
    for section in range(shape[0]):
        speed_sq = base_speed
        for other in range(shape[0]):
            if other != section:
                speed_sq = speed_sq + squares[other]
        coefficient = coefficients(speed_sq, depth, frequency[section])
        current = adjoints[section]
        for sweep in range(SWEEPS):
            extended = jnp.pad(current, ((0, 0), (1, 1), (0, 0)))
            current = relax(neighbours(extended), forcing[section], coefficient)
        adjoints[section] = current
        squares[section] = squared(current)
    return jnp.stack(adjoints)
```

```python
import functools

import jax
import jax.numpy as jnp
from jax import lax
from jax.experimental import pallas as pl
from jax.experimental.pallas import tpu as pltpu
from jax.sharding import PartitionSpec as P

SWEEPS = 16
DRAG_COEF = 0.5
SHIFT_SIGMA = 0.1
ROWS = 16
LANES = 2048
WINDOW = 1152
COLS = WINDOW // 128
SPAN = 3 * ROWS
BOTH = ("con", "tile")


def ring(axis, shift):
    count = lax.axis_size(axis)
    return [(i, (i + shift) % count) for i in range(count)]


def hop_pairs(chip, shift):
    tiles = lax.axis_size("tile")
    return [
        (con * tiles + tile, (con + 2) * tiles + tile + shift)
        for con in (2 * chip, 2 * chip + 1)
        for tile in range(tiles)
        if 0 <= tile + shift < tiles
    ]


def sweep(source, target, gain, offset, lane, first, last):
    for block in range(first, last):
        row = 8 + 8 * block
        inside = pl.ds(8 * block, 8)
        cells = {}

        def rolled(plane, col, shift):
            key = (plane, col % COLS, shift)
            if key not in cells:
                value = source[plane, col % COLS, pl.ds(row, 8), :]
                cells[key] = pltpu.roll(value, shift, 1)
            return cells[key]

        for col in range(COLS):
            total = []
            for plane in range(2):
                up = source[plane, col, pl.ds(row - 1, 8), :]
                down = source[plane, col, pl.ds(row + 1, 8), :]
                left = jnp.where(lane == 0, rolled(plane, col - 1, 1), rolled(plane, col, 1))
                right = jnp.where(
                    lane == 127, rolled(plane, col + 1, 127), rolled(plane, col, 127)
                )
                total.append((up + down) + (left + right))
            gain_real = gain[0, col, inside, :]
            gain_imag = gain[1, col, inside, :]
            target[0, col, pl.ds(row, 8), :] = offset[0, col, inside, :] + (
                gain_real * total[0] - gain_imag * total[1]
            )
            target[1, col, pl.ds(row, 8), :] = offset[1, col, inside, :] + (
                gain_real * total[1] + gain_imag * total[0]
            )


def section_kernel(chip, speeds, carried, *refs):
    count = 3 * speeds + 9 + 1 + (2 if carried else 1)
    ins, (freq_ref,) = refs[: count - 1], refs[count - 1 : count]
    adjoint_ref, sum_ref = refs[count : count + 2]
    next_ref = refs[count + 2] if carried else None
    scratch = refs[count + (3 if carried else 2) :]
    speed_v, field_v, force_v, depth_v, own_v, gain, offset, here, there, out_v, sum_v, sem = scratch
    con = lax.axis_index("con")
    tile = lax.axis_index("tile")
    tiles = lax.axis_size("tile")

    @pl.when(con // 2 == chip)
    def _():
        copies = []
        place = 0
        for term in range(speeds):
            for piece in range(3):
                copies.append((ins[place], speed_v.at[term, piece]))
                place += 1
        for target in (field_v, force_v, depth_v):
            for piece in range(3):
                copies.append((ins[place], target.at[piece]))
                place += 1
        for extra in range(2 if carried else 1):
            copies.append((ins[place], own_v.at[extra]))
            place += 1
        copies = [
            pltpu.make_async_copy(source, target, sem.at[number])
            for number, (source, target) in enumerate(copies)
        ]
        for copy in copies:
            copy.start()
        for copy in copies:
            copy.wait()
        angular = freq_ref[0]
        core = con % 2
        lane = lax.broadcasted_iota(jnp.int32, (8, 128), 1)
        lane2 = lax.broadcasted_iota(jnp.int32, (ROWS, 128), 1)
        nothing = jnp.zeros((8, 128), jnp.float32)
        for col in range(COLS):
            lanes = pl.ds(128 * col, 128)
            for plane in range(2):
                for buffer in (here, there):
                    buffer[plane, col, pl.ds(0, 8), :] = nothing
                    buffer[plane, col, pl.ds(8 + SPAN, 8), :] = nothing
            for piece in range(3):
                speed_sq = speed_v[0, piece, :, lanes]
                if speeds == 2:
                    speed_sq = speed_sq + speed_v[1, piece, :, lanes]
                deep = depth_v[piece, :, lanes]
                drag = DRAG_COEF * jnp.sqrt(speed_sq)
                scaled = deep / (drag * drag + angular * angular)
                gain_real = scaled * drag
                gain_imag = scaled * angular
                diag_real = SHIFT_SIGMA + 4.0 * gain_real
                diag_imag = angular + 4.0 * gain_imag
                inverse = 1.0 / (diag_real * diag_real + diag_imag * diag_imag)
                inv_real = diag_real * inverse
                inv_imag = -diag_imag * inverse
                force_real = force_v[piece, 0, :, lanes]
                force_imag = force_v[piece, 1, :, lanes]
                values = [
                    gain_real * inv_real - gain_imag * inv_imag,
                    gain_real * inv_imag + gain_imag * inv_real,
                    force_real * inv_real - force_imag * inv_imag,
                    force_real * inv_imag + force_imag * inv_real,
                    field_v[piece, 0, :, lanes],
                    field_v[piece, 1, :, lanes],
                ]
                keep = None
                if piece == 0:
                    keep = jnp.broadcast_to(tile > 0, (ROWS, 128))
                if piece == 2:
                    keep = jnp.broadcast_to(tile < tiles - 1, (ROWS, 128))
                edge = None
                if col == 0:
                    edge = (lane2 != 0) | (core == 0)
                if col == COLS - 1:
                    edge = (lane2 != 127) | (core == 1)
                if edge is not None:
                    keep = edge if keep is None else keep & edge
                if keep is not None:
                    values = [jnp.where(keep, value, 0.0) for value in values]
                inside = pl.ds(ROWS * piece, ROWS)
                gain[0, col, inside, :] = values[0]
                gain[1, col, inside, :] = values[1]
                offset[0, col, inside, :] = values[2]
                offset[1, col, inside, :] = values[3]
                here[0, col, pl.ds(8 + ROWS * piece, ROWS), :] = values[4]
                here[1, col, pl.ds(8 + ROWS * piece, ROWS), :] = values[5]

        def both(first, last):
            def step(_, carry):
                sweep(here, there, gain, offset, lane, first, last)
                sweep(there, here, gain, offset, lane, first, last)
                return carry

            return step

        lax.fori_loop(0, SWEEPS // 4, both(0, 6), 0)
        lax.fori_loop(0, SWEEPS // 4, both(1, 5), 0)
        for col in range(COLS):
            lanes = pl.ds(128 * col, 128)
            real = here[0, col, pl.ds(8 + ROWS, ROWS), :]
            imag = here[1, col, pl.ds(8 + ROWS, ROWS), :]
            out_v[0, :, lanes] = real
            out_v[1, :, lanes] = imag
            solved = own_v[0, :, lanes] + (real * real + imag * imag)
            sum_v[0, :, lanes] = solved
            if carried:
                sum_v[1, :, lanes] = solved + own_v[1, :, lanes]
        outs = [(out_v, adjoint_ref), (sum_v.at[0], sum_ref)]
        if carried:
            outs.append((sum_v.at[1], next_ref))
        outs = [
            pltpu.make_async_copy(source, target, sem.at[number])
            for number, (source, target) in enumerate(outs)
        ]
        for copy in outs:
            copy.start()
        for copy in outs:
            copy.wait()


def section(chip, speeds, field, force, deep, own, angular):
    carried = len(own) == 2
    tile_shape = jax.ShapeDtypeStruct((ROWS, WINDOW), jnp.float32)
    pair_shape = jax.ShapeDtypeStruct((2, ROWS, WINDOW), jnp.float32)
    operands = [piece for term in speeds for piece in term] + [*field, *force, *deep, *own]
    anywhere = pl.BlockSpec(memory_space=pl.ANY)
    vmem = lambda *shape: pltpu.VMEM(shape, jnp.float32)
    return pl.pallas_call(
        functools.partial(section_kernel, chip, len(speeds), carried),
        out_shape=[pair_shape, tile_shape] + ([tile_shape] if carried else []),
        in_specs=[anywhere] * len(operands) + [pl.BlockSpec(memory_space=pltpu.SMEM)],
        out_specs=[anywhere] * (3 if carried else 2),
        scratch_shapes=[
            vmem(2, 3, ROWS, WINDOW),
            vmem(3, 2, ROWS, WINDOW),
            vmem(3, 2, ROWS, WINDOW),
            vmem(3, ROWS, WINDOW),
            vmem(2, ROWS, WINDOW),
            vmem(2, COLS, SPAN, 128),
            vmem(2, COLS, SPAN, 128),
            vmem(2, COLS, SPAN + 16, 128),
            vmem(2, COLS, SPAN + 16, 128),
            vmem(2, ROWS, WINDOW),
            vmem(2, ROWS, WINDOW),
            pltpu.SemaphoreType.DMA((len(operands),)),
        ],
        compiler_params=pltpu.CompilerParams(vmem_limit_bytes=16 * 1024 * 1024),
    )(*operands, angular)


def squared(field):
    return field[0] * field[0] + field[1] * field[1]


def beside(value):
    return (
        lax.ppermute(value, "tile", ring("tile", 1)),
        value,
        lax.ppermute(value, "tile", ring("tile", -1)),
    )


def body(first_guess, misfit, innovations, obs_cells, depth, base_speed, frequency):
    chips = lax.axis_size("con") // 2
    con = lax.axis_index("con")
    chip, core = con // 2, con % 2
    swap = [(i, i ^ 1) for i in range(2 * chips)]

    def window(value, side):
        return jnp.where(core == side, value[..., :WINDOW], value[..., -WINDOW:])

    def shared(value):
        mine = window(value, 0)
        got = lax.ppermute(window(value, 1), "con", swap)
        return jnp.where(core == 0, mine, got), jnp.where(core == 0, got, mine)

    field_even, field_odd = shared(first_guess[0])
    lanes = jnp.arange(LANES, dtype=jnp.int32)
    rows = jnp.arange(ROWS, dtype=jnp.int32)
    at_lane = (obs_cells[:, None] % LANES == lanes[None]).astype(jnp.float32)
    at_row = (obs_cells[None] // LANES == rows[:, None]).astype(jnp.float32)
    added = jnp.dot(
        (innovations[0][:, None] * at_row[None]).reshape(2 * ROWS, -1),
        at_lane,
        precision=lax.Precision.HIGHEST,
        preferred_element_type=jnp.float32,
    ).reshape(2, ROWS, LANES)
    force_even, force_odd = shared(misfit[0] + added)
    angular_even, angular_odd = (
        value.reshape(-1)[:1] for value in shared(jnp.broadcast_to(frequency, (8, WINDOW)))
    )
    deep = window(depth, 0)

    square_odd = squared(field_odd)
    square_pair = squared(field_even) + square_odd
    later = window(base_speed, 0)
    for shift in range(1, chips):
        got = lax.ppermute(square_pair, "con", ring("con", -2 * shift))
        later = later + jnp.where(chip + shift < chips, got, 0.0)
    starts = beside(later + square_odd)
    fields_even = beside(field_even)
    forces_even = beside(force_even)
    deeps = beside(deep)
    fields_odd = beside(field_odd)
    forces_odd = beside(force_odd)

    even = jnp.zeros((2, ROWS, WINDOW), jnp.float32)
    odd = even
    passed = None
    for now in range(chips):
        speeds = [starts]
        before = jnp.zeros((ROWS, WINDOW), jnp.float32)
        if passed is not None:
            pieces = [lax.ppermute(passed, BOTH, hop_pairs(now - 1, shift)) for shift in (1, 0, -1)]
            speeds.append(pieces)
            before = pieces[1]
        solved, passed, speed = section(
            now, speeds, fields_even, forces_even, deeps, [before, later], angular_even
        )
        even = jnp.where(chip == now, solved, even)
        solved, passed = section(
            now, [beside(speed)], fields_odd, forces_odd, deeps, [passed], angular_odd
        )
        odd = jnp.where(chip == now, solved, odd)

    own = LANES // 2
    sent = jnp.where(core == 0, odd[..., :own], even[..., -own:])
    got = lax.ppermute(sent, "con", swap)
    result = jnp.where(
        core == 0,
        jnp.concatenate([even[..., :own], got], axis=-1),
        jnp.concatenate([got, odd[..., -own:]], axis=-1),
    )
    return result[None]


def solution(mesh):
    placed = (
        P("con", None, "tile", None),
        P("con", None, "tile", None),
        P("con", None, "tile"),
        P("tile"),
        P("tile", None),
        P("tile", None),
        P("con"),
    )
    return jax.shard_map(
        body, mesh=mesh, in_specs=placed, out_specs=P("con", None, "tile", None), check_vma=False
    )
```

```python
import functools

import jax
import jax.numpy as jnp
from jax import lax
from jax.experimental import pallas as pl
from jax.experimental.pallas import tpu as pltpu
from jax.sharding import PartitionSpec as P

SWEEPS = 16
DRAG_COEF = 0.5
SHIFT_SIGMA = 0.1
ROWS = 16
LANES = 2048
WINDOW = 1152
COLS = WINDOW // 128
SPAN = 3 * ROWS
BOTH = ("con", "tile")


def ring(axis, shift):
    count = lax.axis_size(axis)
    return [(i, (i + shift) % count) for i in range(count)]


def hop_pairs(chip, shift):
    tiles = lax.axis_size("tile")
    return [
        (con * tiles + tile, (con + 2) * tiles + tile + shift)
        for con in (2 * chip, 2 * chip + 1)
        for tile in range(tiles)
        if 0 <= tile + shift < tiles
    ]


def sweep(source, target, gain, offset, lane, base, blocks):
    for block in range(blocks):
        inside = pl.ds(base + 8 * block, 8)
        middle = pl.ds(8 + base + 8 * block, 8)
        above = pl.ds(7 + base + 8 * block, 8)
        below = pl.ds(9 + base + 8 * block, 8)
        cells = {}

        def rolled(plane, col, shift):
            key = (plane, col % COLS, shift)
            if key not in cells:
                cells[key] = pltpu.roll(source[plane, col % COLS, middle, :], shift, 1)
            return cells[key]

        for col in range(COLS):
            total = []
            for plane in range(2):
                along = source[plane, col, above, :] + source[plane, col, below, :]
                left = jnp.where(lane == 0, rolled(plane, col - 1, 1), rolled(plane, col, 1))
                right = jnp.where(
                    lane == 127, rolled(plane, col + 1, 127), rolled(plane, col, 127)
                )
                total.append(along + (left + right))
            gain_real = gain[0, col, inside, :]
            gain_imag = gain[1, col, inside, :]
            target[0, col, middle, :] = offset[0, col, inside, :] + (
                gain_real * total[0] - gain_imag * total[1]
            )
            target[1, col, middle, :] = offset[1, col, inside, :] + (
                gain_real * total[1] + gain_imag * total[0]
            )


def section_kernel(chip, speeds, carried, more, *refs):
    refs = list(refs)
    take = lambda count: [refs.pop(0) for _ in range(count)]
    speed_refs = [take(3) for _ in range(speeds)]
    field_refs, deep_refs = take(3), take(3)
    (tone_ref,) = take(1)
    passed_ref = take(1)[0] if carried else None
    later_ref = take(1)[0] if more else None
    adjoint_out, passed_out = take(2)
    speed_out = take(1)[0] if more else None
    gain, offset, here, there = refs
    con = lax.axis_index("con")
    tile = lax.axis_index("tile")
    tiles = lax.axis_size("tile")
    core = con % 2

    @pl.when(con // 2 == chip)
    def _():
        lane = lax.broadcasted_iota(jnp.int32, (8, 128), 1)
        lane2 = lax.broadcasted_iota(jnp.int32, (ROWS, 128), 1)
        nothing = jnp.zeros((8, 128), jnp.float32)
        angular = jnp.broadcast_to(tone_ref[0:1, 0:128], (ROWS, 128))
        for col in range(COLS):
            lanes = pl.ds(128 * col, 128)
            for buffer in (here, there):
                for plane in range(2):
                    buffer[plane, col, pl.ds(0, 8), :] = nothing
                    buffer[plane, col, pl.ds(8 + SPAN, 8), :] = nothing
            for piece in range(3):
                speed_sq = speed_refs[0][piece][:, lanes]
                if speeds == 2:
                    speed_sq = speed_sq + speed_refs[1][piece][:, lanes]
                deep = deep_refs[piece][pl.ds(4 * ROWS, ROWS), lanes]
                drag = DRAG_COEF * jnp.sqrt(speed_sq)
                scaled = deep / (drag * drag + angular * angular)
                gain_real = scaled * drag
                gain_imag = scaled * angular
                diag_real = SHIFT_SIGMA + 4.0 * gain_real
                diag_imag = angular + 4.0 * gain_imag
                inverse = 1.0 / (diag_real * diag_real + diag_imag * diag_imag)
                inv_real = diag_real * inverse
                inv_imag = -diag_imag * inverse
                field_real, field_imag, force_real, force_imag = (
                    field_refs[piece][pl.ds(ROWS * part, ROWS), lanes] for part in range(4)
                )
                values = [
                    gain_real * inv_real - gain_imag * inv_imag,
                    gain_real * inv_imag + gain_imag * inv_real,
                    force_real * inv_real - force_imag * inv_imag,
                    force_real * inv_imag + force_imag * inv_real,
                    field_real,
                    field_imag,
                ]
                keep = None
                if piece == 0:
                    keep = jnp.broadcast_to(tile > 0, (ROWS, 128))
                if piece == 2:
                    keep = jnp.broadcast_to(tile < tiles - 1, (ROWS, 128))
                edge = None
                if col == 0:
                    edge = (lane2 != 0) | (core == 0)
                if col == COLS - 1:
                    edge = (lane2 != 127) | (core == 1)
                if edge is not None:
                    keep = edge if keep is None else keep & edge
                if keep is not None:
                    values = [jnp.where(keep, value, 0.0) for value in values]
                inside = pl.ds(ROWS * piece, ROWS)
                shifted = pl.ds(8 + ROWS * piece, ROWS)
                gain[0, col, inside, :] = values[0]
                gain[1, col, inside, :] = values[1]
                offset[0, col, inside, :] = values[2]
                offset[1, col, inside, :] = values[3]
                here[0, col, shifted, :] = values[4]
                here[1, col, shifted, :] = values[5]

        for phase in range(4):

            def step(_, carry):
                sweep(here, there, gain, offset, lane, 4 * phase, 6 - phase)
                sweep(there, here, gain, offset, lane, 4 * phase, 6 - phase)
                return carry

            lax.fori_loop(0, SWEEPS // 8, step, 0)
        for col in range(COLS):
            lanes = pl.ds(128 * col, 128)
            real = here[0, col, pl.ds(8 + ROWS, ROWS), :]
            imag = here[1, col, pl.ds(8 + ROWS, ROWS), :]
            adjoint_out[0, :, lanes] = real
            adjoint_out[1, :, lanes] = imag
            total = real * real + imag * imag
            if carried:
                total = total + passed_ref[:, lanes]
            passed_out[:, lanes] = total
            if more:
                speed_out[:, lanes] = total + later_ref[:, lanes]


def section(chip, speeds, fields, deeps, tone, passed=None, later=None):
    tile_shape = jax.ShapeDtypeStruct((ROWS, WINDOW), jnp.float32)
    pair_shape = jax.ShapeDtypeStruct((2, ROWS, WINDOW), jnp.float32)
    operands = [piece for term in speeds for piece in term] + [*fields, *deeps, tone]
    operands += [value for value in (passed, later) if value is not None]
    outs = [pair_shape, tile_shape] + ([tile_shape] if later is not None else [])
    whole = pl.BlockSpec(memory_space=pltpu.VMEM)
    vmem = lambda rows: pltpu.VMEM((2, COLS, rows, 128), jnp.float32)
    return pl.pallas_call(
        functools.partial(
            section_kernel, chip, len(speeds), passed is not None, later is not None
        ),
        out_shape=outs,
        in_specs=[whole] * len(operands),
        out_specs=[whole] * len(outs),
        scratch_shapes=[vmem(SPAN), vmem(SPAN), vmem(SPAN + 16), vmem(SPAN + 16)],
        compiler_params=pltpu.CompilerParams(vmem_limit_bytes=24 * 1024 * 1024),
    )(*operands)


def squared(field):
    return field[0] * field[0] + field[1] * field[1]


def beside(value):
    return (
        lax.ppermute(value, "tile", ring("tile", 1)),
        value,
        lax.ppermute(value, "tile", ring("tile", -1)),
    )


def after(value, *others):
    return lax.optimization_barrier((value, *others))[0]


def body(first_guess, misfit, innovations, obs_cells, depth, base_speed, frequency):
    chips = lax.axis_size("con") // 2
    con = lax.axis_index("con")
    chip, core = con // 2, con % 2
    swap = [(i, i ^ 1) for i in range(2 * chips)]

    def window(value, side):
        return jnp.where(core == side, value[..., :WINDOW], value[..., -WINDOW:])

    def shared(value):
        mine, sent = window(value, 0), window(value, 1)
        got = lax.ppermute(sent, "con", swap)
        return jnp.where(core == 0, mine, got), jnp.where(core == 0, got, mine), sent

    field_even, field_odd, sent = shared(first_guess[0])
    square_odd = squared(field_odd)
    square_pair = squared(field_even) + square_odd
    later = window(base_speed, 0)
    for shift in range(1, chips):
        got = lax.ppermute(square_pair, "con", ring("con", -2 * shift))
        later = later + jnp.where(chip + shift < chips, got, 0.0)
    starts = beside(later + square_odd)

    innovations = after(innovations, sent)
    lanes = jnp.arange(LANES, dtype=jnp.int32)
    rows = jnp.arange(ROWS, dtype=jnp.int32)
    at_lane = (obs_cells[:, None] % LANES == lanes[None]).astype(jnp.float32)
    at_row = (obs_cells[None] // LANES == rows[:, None]).astype(jnp.float32)
    added = jnp.dot(
        (innovations[0][:, None] * at_row[None]).reshape(2 * ROWS, -1),
        at_lane,
        precision=lax.Precision.HIGHEST,
        preferred_element_type=jnp.float32,
    )
    forcing = misfit[0].reshape(2 * ROWS, LANES) + added
    tones = jnp.broadcast_to(frequency, (8, LANES))
    force_even, force_odd, _ = shared(jnp.concatenate([forcing, tones]))
    tone_even, tone_odd = force_even[2 * ROWS :], force_odd[2 * ROWS :]
    flat = lambda field: field.reshape(2 * ROWS, WINDOW)
    evens = beside(
        jnp.concatenate([flat(field_even), force_even[: 2 * ROWS], window(depth, 0)])
    )
    odds = beside(jnp.concatenate([flat(after(field_odd, starts[0], starts[2], evens[0], evens[2])), force_odd[: 2 * ROWS]]))

    even = odd = passed = None
    for now in range(chips):
        speeds = [starts]
        if now:
            up, down, passed = [
                lax.ppermute(passed, BOTH, hop_pairs(now - 1, shift)) for shift in (1, -1, 0)
            ]
            speeds.append([up, passed, down])
        solved, passed, speed = section(now, speeds, evens, evens, tone_even, passed, later)
        even = solved if even is None else jnp.where(chip == now, solved, even)
        solved, passed = section(now, [beside(speed)], odds, evens, tone_odd, passed)
        odd = solved if odd is None else jnp.where(chip == now, solved, odd)

    own = LANES // 2
    sent = jnp.where(core == 0, odd[..., :own], even[..., -own:])
    got = lax.ppermute(sent, "con", swap)
    result = jnp.where(
        core == 0,
        jnp.concatenate([even[..., :own], got], axis=-1),
        jnp.concatenate([got, odd[..., -own:]], axis=-1),
    )
    return result[None]


def solution(mesh):
    placed = (
        P("con", None, "tile", None),
        P("con", None, "tile", None),
        P("con", None, "tile"),
        P("tile"),
        P("tile", None),
        P("tile", None),
        P("con"),
    )
    return jax.shard_map(
        body, mesh=mesh, in_specs=placed, out_specs=P("con", None, "tile", None), check_vma=False
    )
```

```python
import functools

import jax
import jax.numpy as jnp
from jax import lax
from jax.experimental import pallas as pl
from jax.experimental.pallas import tpu as pltpu
from jax.sharding import PartitionSpec as P

SWEEPS = 16
DRAG_COEF = 0.5
SHIFT_SIGMA = 0.1
ROWS = 16
LANES = 2048
WINDOW = 1152
COLS = WINDOW // 128
SPAN = 3 * ROWS
BOTH = ("con", "tile")


def hop_pairs(chip, shift):
    tiles = lax.axis_size("tile")
    return [
        (con * tiles + tile, (con + 2) * tiles + tile + step)
        for con, step in ((2 * chip, shift), (2 * chip + 1, -shift))
        for tile in range(tiles)
        if 0 <= tile + step < tiles
    ]


def sweep(source, target, gain, offset, base, blocks):
    for block in range(blocks):
        inside = pl.ds(base + 8 * block, 8)
        middle = pl.ds(8 + base + 8 * block, 8)
        above = pl.ds(7 + base + 8 * block, 8)
        below = pl.ds(9 + base + 8 * block, 8)
        cells = {
            (plane, col): source[plane, col, middle, :] for plane in range(2) for col in range(COLS)
        }
        for plane in range(2):
            cells[plane, -1] = pltpu.roll(cells[plane, COLS - 1], 1, 1)
            cells[plane, COLS] = pltpu.roll(cells[plane, 0], 127, 1)

        for col in range(COLS):
            total = []
            for plane in range(2):
                along = source[plane, col, above, :] + source[plane, col, below, :]
                across = cells[plane, col - 1] + cells[plane, col + 1]
                total.append(along + across)
            gain_real = gain[0, col, inside, :]
            gain_imag = gain[1, col, inside, :]
            target[0, col, middle, :] = offset[0, col, inside, :] + (
                gain_real * total[0] - gain_imag * total[1]
            )
            target[1, col, middle, :] = offset[1, col, inside, :] + (
                gain_real * total[1] + gain_imag * total[0]
            )


def section_kernel(chip, speeds, carried, more, *refs):
    refs = list(refs)
    take = lambda count: [refs.pop(0) for _ in range(count)]
    speed_refs = [take(3) for _ in range(speeds)]
    field_refs, deep_refs = take(3), take(3)
    (tone_ref,) = take(1)
    passed_ref = take(1)[0] if carried else None
    later_ref = take(1)[0] if more else None
    adjoint_out, passed_out = take(2)
    speed_out = take(1)[0] if more else None
    gain, offset, here, there = refs
    con = lax.axis_index("con")
    tile = lax.axis_index("tile")
    tiles = lax.axis_size("tile")
    core = con % 2

    @pl.when(con // 2 == chip)
    def _():
        lane2 = lax.broadcasted_iota(jnp.int32, (ROWS, 128), 1)
        nothing = jnp.zeros((8, 128), jnp.float32)
        angular = jnp.broadcast_to(tone_ref[0:1, 0:128], (ROWS, 128))
        first_row = pl.multiple_of(2 * ROWS * core, ROWS)
        places = (first_row, ROWS, pl.multiple_of(2 * ROWS - first_row, ROWS))
        above, below = tile > 0, tile < tiles - 1
        inner = [
            jnp.logical_or(
                jnp.logical_and(core == turn, above), jnp.logical_and(core != turn, below)
            )
            for turn in range(2)
        ]
        for col in range(COLS):
            lanes = pl.ds(128 * col, 128)
            for buffer in (here, there):
                for plane in range(2):
                    buffer[plane, col, pl.ds(0, 8), :] = nothing
                    buffer[plane, col, pl.ds(8 + SPAN, 8), :] = nothing
            for piece in range(3):
                speed_sq = speed_refs[0][piece][:, lanes]
                if speeds == 2:
                    speed_sq = speed_sq + speed_refs[1][piece][:, lanes]
                deep = deep_refs[piece][pl.ds(4 * ROWS, ROWS), lanes]
                drag = DRAG_COEF * jnp.sqrt(speed_sq)
                scaled = deep / (drag * drag + angular * angular)
                gain_real = scaled * drag
                gain_imag = scaled * angular
                diag_real = SHIFT_SIGMA + 4.0 * gain_real
                diag_imag = angular + 4.0 * gain_imag
                inverse = 1.0 / (diag_real * diag_real + diag_imag * diag_imag)
                inv_real = diag_real * inverse
                inv_imag = -diag_imag * inverse
                field_real, field_imag, force_real, force_imag = (
                    field_refs[piece][pl.ds(ROWS * part, ROWS), lanes] for part in range(4)
                )
                values = [
                    gain_real * inv_real - gain_imag * inv_imag,
                    gain_real * inv_imag + gain_imag * inv_real,
                    force_real * inv_real - force_imag * inv_imag,
                    force_real * inv_imag + force_imag * inv_real,
                    field_real,
                    field_imag,
                ]
                keep = None
                if piece != 1:
                    keep = jnp.broadcast_to(inner[piece // 2], (ROWS, 128))
                edge = None
                if col == 0:
                    edge = (lane2 != 0) | (core == 0)
                if col == COLS - 1:
                    edge = (lane2 != 127) | (core == 1)
                if edge is not None:
                    keep = edge if keep is None else keep & edge
                if keep is not None:
                    values = [jnp.where(keep, value, 0.0) for value in values]
                inside = pl.ds(places[piece], ROWS)
                shifted = pl.ds(8 + places[piece], ROWS)
                gain[0, col, inside, :] = values[0]
                gain[1, col, inside, :] = values[1]
                offset[0, col, inside, :] = values[2]
                offset[1, col, inside, :] = values[3]
                here[0, col, shifted, :] = values[4]
                here[1, col, shifted, :] = values[5]

        for phase in range(4):

            def step(_, carry):
                sweep(here, there, gain, offset, 4 * phase, 6 - phase)
                sweep(there, here, gain, offset, 4 * phase, 6 - phase)
                return carry

            lax.fori_loop(0, SWEEPS // 8, step, 0)
        for col in range(COLS):
            lanes = pl.ds(128 * col, 128)
            real = here[0, col, pl.ds(8 + ROWS, ROWS), :]
            imag = here[1, col, pl.ds(8 + ROWS, ROWS), :]
            adjoint_out[0, :, lanes] = real
            adjoint_out[1, :, lanes] = imag
            total = real * real + imag * imag
            if carried:
                total = total + passed_ref[:, lanes]
            passed_out[:, lanes] = total
            if more:
                speed_out[:, lanes] = total + later_ref[:, lanes]


def section(chip, speeds, fields, deeps, tone, passed=None, later=None):
    tile_shape = jax.ShapeDtypeStruct((ROWS, WINDOW), jnp.float32)
    pair_shape = jax.ShapeDtypeStruct((2, ROWS, WINDOW), jnp.float32)
    operands = [piece for term in speeds for piece in term] + [*fields, *deeps, tone]
    operands += [value for value in (passed, later) if value is not None]
    outs = [pair_shape, tile_shape] + ([tile_shape] if later is not None else [])
    whole = pl.BlockSpec(memory_space=pltpu.VMEM)
    vmem = lambda rows: pltpu.VMEM((2, COLS, rows, 128), jnp.float32)
    return pl.pallas_call(
        functools.partial(
            section_kernel, chip, len(speeds), passed is not None, later is not None
        ),
        out_shape=outs,
        in_specs=[whole] * len(operands),
        out_specs=[whole] * len(outs),
        scratch_shapes=[vmem(SPAN), vmem(SPAN), vmem(SPAN + 16), vmem(SPAN + 16)],
        compiler_params=pltpu.CompilerParams(vmem_limit_bytes=24 * 1024 * 1024),
    )(*operands)


def weave(blocks, store, turned):
    rows = blocks[0].shape[0]
    for col in range(COLS):
        turned[pl.ds(128 * col, 128), pl.ds(0, rows)] = blocks[col].T
    for col in range(COLS):
        store(col, turned[pl.ds(col, 128, stride=COLS), pl.ds(0, rows)].T)


def weave_kernel(groups, *refs):
    refs = list(refs)
    turned = refs.pop()
    outs = refs[-len(groups) :]
    for group, out in zip(groups, outs):
        parts = [(refs.pop(0), rows) for rows in group]
        blocks = [
            jnp.concatenate(
                [part[pl.ds(0, rows), pl.ds(128 * col, 128)] for part, rows in parts], axis=0
            )
            for col in range(COLS)
        ]

        def store(col, value):
            out[:, pl.ds(128 * col, 128)] = value

        weave(blocks, store, turned)


def woven(*groups):
    whole = pl.BlockSpec(memory_space=pltpu.VMEM)
    sizes = [[rows for _, rows in group] for group in groups]
    operands = [value for group in groups for value, _ in group]
    return pl.pallas_call(
        functools.partial(weave_kernel, sizes),
        out_shape=[jax.ShapeDtypeStruct((sum(rows), WINDOW), jnp.float32) for rows in sizes],
        in_specs=[whole] * len(operands),
        out_specs=[whole] * len(groups),
        scratch_shapes=[pltpu.VMEM((WINDOW, 128), jnp.float32)],
        compiler_params=pltpu.CompilerParams(vmem_limit_bytes=24 * 1024 * 1024),
    )(*operands)


def unweave_kernel(*refs):
    refs = list(refs)
    kept_out, sent_out, even_turned, odd_turned = refs[-4:]
    evens, odds = refs[:-4][0::2], refs[:-4][1::2]
    con = lax.axis_index("con")
    chip, core = con // 2, con % 2
    for pieces, turned in ((evens, even_turned), (odds, odd_turned)):
        for col in range(COLS):
            lanes = pl.ds(128 * col, 128)
            value = None
            for place, piece in enumerate(pieces):
                block = jnp.concatenate([piece[0, :, lanes], piece[1, :, lanes]], axis=0)
                value = block if value is None else jnp.where(chip == place, block, value)
            turned[pl.ds(col, 128, stride=COLS), pl.ds(0, 2 * ROWS)] = value.T
    for col in range(COLS - 1):
        lanes = pl.ds(128 * col, 128)

        def straight(turned, at):
            return turned[pl.ds(128 * at, 128), pl.ds(0, 2 * ROWS)]

        kept = jnp.where(core == 0, straight(even_turned, col), straight(odd_turned, col + 1)).T
        sent = jnp.where(core == 0, straight(odd_turned, col), straight(even_turned, col + 1)).T
        for plane in range(2):
            rows = slice(ROWS * plane, ROWS * (plane + 1))
            kept_out[plane, :, lanes] = kept[rows]
            sent_out[plane, :, lanes] = sent[rows]


def unwoven(pieces):
    whole = pl.BlockSpec(memory_space=pltpu.VMEM)
    half = jax.ShapeDtypeStruct((2, ROWS, LANES // 2), jnp.float32)
    return pl.pallas_call(
        unweave_kernel,
        out_shape=[half, half],
        in_specs=[whole] * len(pieces),
        out_specs=[whole, whole],
        scratch_shapes=[pltpu.VMEM((WINDOW, 128), jnp.float32)] * 2,
        compiler_params=pltpu.CompilerParams(vmem_limit_bytes=24 * 1024 * 1024),
    )(*pieces)


def squared(field):
    return field[0] * field[0] + field[1] * field[1]


def snake(turn):
    cons, tiles = lax.axis_size("con"), lax.axis_size("tile")
    pairs = []
    for con in range(cons):
        for tile in range(tiles):
            there = tile + (1 if con % 2 == turn else -1)
            other = (con, there) if 0 <= there < tiles else (con ^ 1, tile)
            pairs.append((con * tiles + tile, other[0] * tiles + other[1]))
    return pairs


def beside(value):
    return (
        lax.ppermute(value, BOTH, snake(0)),
        value,
        lax.ppermute(value, BOTH, snake(1)),
    )


def after(value, *others):
    return lax.optimization_barrier((value, *others))[0]


def body(first_guess, misfit, innovations, obs_cells, depth, base_speed, frequency):
    chips = lax.axis_size("con") // 2
    con = lax.axis_index("con")
    chip, core = con // 2, con % 2
    swap = [(i, i ^ 1) for i in range(2 * chips)]

    def window(value, side):
        return jnp.where(core == side, value[..., :WINDOW], value[..., -WINDOW:])

    def shared(value):
        mine, sent = window(value, 0), window(value, 1)
        got = lax.ppermute(sent, "con", swap)
        return jnp.where(core == 0, mine, got), jnp.where(core == 0, got, mine), sent

    field_even, field_odd, sent = shared(first_guess[0])
    square_odd = squared(field_odd)
    square_pair = squared(field_even) + square_odd
    later = window(base_speed, 0)
    for step in range(1, chips):
        pairs = [(i, i ^ (2 * step)) for i in range(2 * chips)]
        got = lax.ppermute(square_pair, "con", pairs)
        later = later + jnp.where(chip ^ step > chip, got, 0.0)
    start, later = woven([(later + square_odd, ROWS)], [(later, ROWS)])
    starts = beside(start)

    innovations = after(innovations, sent)
    lanes = jnp.arange(LANES, dtype=jnp.int32)
    rows = jnp.arange(ROWS, dtype=jnp.int32)
    at_lane = (obs_cells[:, None] % LANES == lanes[None]).astype(jnp.float32)
    at_row = (obs_cells[None] // LANES == rows[:, None]).astype(jnp.float32)
    added = jnp.dot(
        (innovations[0][:, None] * at_row[None]).reshape(2 * ROWS, -1),
        at_lane,
        precision=lax.Precision.HIGHEST,
        preferred_element_type=jnp.float32,
    )
    forcing = misfit[0].reshape(2 * ROWS, LANES) + added
    tones = jnp.broadcast_to(frequency, (8, LANES))
    force_even, force_odd, _ = shared(jnp.concatenate([forcing, tones]))
    tone_even, tone_odd = force_even[2 * ROWS :], force_odd[2 * ROWS :]
    flat = lambda field: field.reshape(2 * ROWS, WINDOW)
    even_bundle, odd_bundle = woven(
        [(flat(field_even), 2 * ROWS), (force_even, 2 * ROWS), (window(depth, 0), ROWS)],
        [(flat(field_odd), 2 * ROWS), (force_odd, 2 * ROWS)],
    )
    evens = beside(even_bundle)
    odds = beside(after(odd_bundle, starts[0], starts[2], evens[0], evens[2]))

    passed, results = None, []
    for now in range(chips):
        speeds = [starts]
        if now:
            up, down, passed = [
                lax.ppermute(passed, BOTH, hop_pairs(now - 1, shift)) for shift in (1, -1, 0)
            ]
            speeds.append([up, passed, down])
        solved, passed, speed = section(now, speeds, evens, evens, tone_even, passed, later)
        results.append(solved)
        solved, passed = section(now, [beside(speed)], odds, evens, tone_odd, passed)
        results.append(solved)

    kept, sent = unwoven(results)
    got = lax.ppermute(sent, "con", swap)
    result = jnp.where(
        core == 0,
        jnp.concatenate([kept, got], axis=-1),
        jnp.concatenate([got, kept], axis=-1),
    )
    return result[None]


def solution(mesh):
    placed = (
        P("con", None, "tile", None),
        P("con", None, "tile", None),
        P("con", None, "tile"),
        P("tile"),
        P("tile", None),
        P("tile", None),
        P("con"),
    )
    return jax.shard_map(
        body, mesh=mesh, in_specs=placed, out_specs=P("con", None, "tile", None), check_vma=False
    )
```

```python
import functools

import jax
import jax.numpy as jnp
from jax import lax
from jax.experimental import pallas as pl
from jax.experimental.pallas import tpu as pltpu
from jax.sharding import PartitionSpec as P

SWEEPS = 16
DRAG_COEF = 0.5
SHIFT_SIGMA = 0.1
ROWS = 16
LANES = 2048
WINDOW = 1152
COLS = WINDOW // 128
SPAN = 3 * ROWS
BOTH = ("con", "tile")


def hop_pairs(chip, shift):
    tiles = lax.axis_size("tile")
    return [
        (con * tiles + tile, (con + 2) * tiles + tile + step)
        for con, step in ((2 * chip, -shift), (2 * chip + 1, shift))
        for tile in range(tiles)
        if 0 <= tile + step < tiles
    ]


def sweep(source, target, gain, offset, base, blocks):
    for block in range(blocks):
        inside = pl.ds(base + 8 * block, 8)
        middle = pl.ds(8 + base + 8 * block, 8)
        above = pl.ds(7 + base + 8 * block, 8)
        below = pl.ds(9 + base + 8 * block, 8)
        cells = {
            (plane, col): source[plane, col, middle, :] for plane in range(2) for col in range(COLS)
        }
        for plane in range(2):
            cells[plane, -1] = pltpu.roll(cells[plane, COLS - 1], 1, 1)
            cells[plane, COLS] = pltpu.roll(cells[plane, 0], 127, 1)

        for col in range(COLS):
            total = []
            for plane in range(2):
                along = source[plane, col, above, :] + source[plane, col, below, :]
                across = cells[plane, col - 1] + cells[plane, col + 1]
                total.append(along + across)
            gain_real = gain[0, col, inside, :]
            gain_imag = gain[1, col, inside, :]
            target[0, col, middle, :] = offset[0, col, inside, :] + (
                gain_real * total[0] - gain_imag * total[1]
            )
            target[1, col, middle, :] = offset[1, col, inside, :] + (
                gain_real * total[1] + gain_imag * total[0]
            )


def section_kernel(chip, speeds, carried, more, first, *refs):
    refs = list(refs)
    take = lambda count: [refs.pop(0) for _ in range(count)]
    speed_refs = [take(3) for _ in range(speeds)]
    field_refs, force_refs = take(3), take(3)
    (tone_ref,) = take(1)
    passed_ref = take(1)[0] if carried else None
    later_ref = take(1)[0] if more else None
    adjoint_out, passed_out = take(2)
    speed_out = take(1)[0] if more else None
    gain, offset, here, there = refs
    con = lax.axis_index("con")
    tile = lax.axis_index("tile")
    tiles = lax.axis_size("tile")
    core = con % 2

    @pl.when(con // 2 == chip)
    def _():
        lane2 = lax.broadcasted_iota(jnp.int32, (ROWS, 128), 1)
        nothing = jnp.zeros((8, 128), jnp.float32)
        angular = jnp.broadcast_to(tone_ref[0:1, 0:128], (ROWS, 128))
        first_row = pl.multiple_of(2 * ROWS * (1 - core), ROWS)
        places = (first_row, ROWS, pl.multiple_of(2 * ROWS - first_row, ROWS))
        above, below = tile > 0, tile < tiles - 1
        inner = [
            jnp.logical_or(
                jnp.logical_and(core != turn, above), jnp.logical_and(core == turn, below)
            )
            for turn in range(2)
        ]
        for col in range(COLS):
            lanes = pl.ds(128 * col, 128)
            for buffer in (here, there):
                for plane in range(2):
                    buffer[plane, col, pl.ds(0, 8), :] = nothing
                    buffer[plane, col, pl.ds(8 + SPAN, 8), :] = nothing
            for piece in range(3):
                speed_sq = speed_refs[0][piece][:, lanes]
                if speeds == 2:
                    speed_sq = speed_sq + speed_refs[1][piece][:, lanes]
                deep = force_refs[piece][pl.ds(4 * ROWS, ROWS), lanes]
                drag = DRAG_COEF * jnp.sqrt(speed_sq)
                scaled = deep / (drag * drag + angular * angular)
                gain_real = scaled * drag
                gain_imag = scaled * angular
                diag_real = SHIFT_SIGMA + 4.0 * gain_real
                diag_imag = angular + 4.0 * gain_imag
                inverse = 1.0 / (diag_real * diag_real + diag_imag * diag_imag)
                inv_real = diag_real * inverse
                inv_imag = -diag_imag * inverse
                field_real, field_imag, force_real, force_imag = (
                    part[piece][pl.ds(first + ROWS * plane, ROWS), lanes]
                    for part in (field_refs, force_refs)
                    for plane in range(2)
                )
                values = [
                    gain_real * inv_real - gain_imag * inv_imag,
                    gain_real * inv_imag + gain_imag * inv_real,
                    force_real * inv_real - force_imag * inv_imag,
                    force_real * inv_imag + force_imag * inv_real,
                    field_real,
                    field_imag,
                ]
                keep = None
                if piece != 1:
                    keep = jnp.broadcast_to(inner[piece // 2], (ROWS, 128))
                edge = None
                if col == 0:
                    edge = (lane2 != 0) | (core == 0)
                if col == COLS - 1:
                    edge = (lane2 != 127) | (core == 1)
                if edge is not None:
                    keep = edge if keep is None else keep & edge
                if keep is not None:
                    values = [jnp.where(keep, value, 0.0) for value in values]
                inside = pl.ds(places[piece], ROWS)
                shifted = pl.ds(8 + places[piece], ROWS)
                gain[0, col, inside, :] = values[0]
                gain[1, col, inside, :] = values[1]
                offset[0, col, inside, :] = values[2]
                offset[1, col, inside, :] = values[3]
                here[0, col, shifted, :] = values[4]
                here[1, col, shifted, :] = values[5]

        for phase in range(4):

            def step(_, carry):
                sweep(here, there, gain, offset, 4 * phase, 6 - phase)
                sweep(there, here, gain, offset, 4 * phase, 6 - phase)
                return carry

            lax.fori_loop(0, SWEEPS // 8, step, 0)
        for col in range(COLS):
            lanes = pl.ds(128 * col, 128)
            real = here[0, col, pl.ds(8 + ROWS, ROWS), :]
            imag = here[1, col, pl.ds(8 + ROWS, ROWS), :]
            adjoint_out[0, :, lanes] = real
            adjoint_out[1, :, lanes] = imag
            total = real * real + imag * imag
            if carried:
                total = total + passed_ref[:, lanes]
            passed_out[:, lanes] = total
            if more:
                speed_out[:, lanes] = total + later_ref[:, lanes]


def section(chip, speeds, fields, forces, first, tone, passed=None, later=None):
    tile_shape = jax.ShapeDtypeStruct((ROWS, WINDOW), jnp.float32)
    pair_shape = jax.ShapeDtypeStruct((2, ROWS, WINDOW), jnp.float32)
    operands = [piece for term in speeds for piece in term] + [*fields, *forces, tone]
    operands += [value for value in (passed, later) if value is not None]
    outs = [pair_shape, tile_shape] + ([tile_shape] if later is not None else [])
    whole = pl.BlockSpec(memory_space=pltpu.VMEM)
    vmem = lambda rows: pltpu.VMEM((2, COLS, rows, 128), jnp.float32)
    return pl.pallas_call(
        functools.partial(
            section_kernel, chip, len(speeds), passed is not None, later is not None, first
        ),
        out_shape=outs,
        in_specs=[whole] * len(operands),
        out_specs=[whole] * len(outs),
        scratch_shapes=[vmem(SPAN), vmem(SPAN), vmem(SPAN + 16), vmem(SPAN + 16)],
        compiler_params=pltpu.CompilerParams(vmem_limit_bytes=24 * 1024 * 1024),
    )(*operands)


def weave(blocks, store, turned):
    rows = blocks[0].shape[0]
    for col in range(COLS):
        turned[pl.ds(128 * col, 128), pl.ds(0, rows)] = blocks[col].T
    for col in range(COLS):
        store(col, turned[pl.ds(col, 128, stride=COLS), pl.ds(0, rows)].T)


def weave_kernel(groups, *refs):
    refs = list(refs)
    turned = refs.pop()
    outs = refs[-len(groups) :]
    for group, out in zip(groups, outs):
        parts = [(refs.pop(0), rows) for rows in group]
        blocks = [
            jnp.concatenate(
                [part[pl.ds(0, rows), pl.ds(128 * col, 128)] for part, rows in parts], axis=0
            )
            for col in range(COLS)
        ]

        def store(col, value):
            out[:, pl.ds(128 * col, 128)] = value

        weave(blocks, store, turned)


def woven(*groups):
    whole = pl.BlockSpec(memory_space=pltpu.VMEM)
    sizes = [[rows for _, rows in group] for group in groups]
    operands = [value for group in groups for value, _ in group]
    return pl.pallas_call(
        functools.partial(weave_kernel, sizes),
        out_shape=[jax.ShapeDtypeStruct((sum(rows), WINDOW), jnp.float32) for rows in sizes],
        in_specs=[whole] * len(operands),
        out_specs=[whole] * len(groups),
        scratch_shapes=[pltpu.VMEM((WINDOW, 128), jnp.float32)],
        compiler_params=pltpu.CompilerParams(vmem_limit_bytes=24 * 1024 * 1024),
    )(*operands)


def unweave_kernel(*refs):
    refs = list(refs)
    kept_out, sent_out, even_turned, odd_turned = refs[-4:]
    evens, odds = refs[:-4][0::2], refs[:-4][1::2]
    con = lax.axis_index("con")
    chip, core = con // 2, con % 2
    for pieces, turned in ((evens, even_turned), (odds, odd_turned)):
        for col in range(COLS):
            lanes = pl.ds(128 * col, 128)
            value = None
            for place, piece in enumerate(pieces):
                block = jnp.concatenate([piece[0, :, lanes], piece[1, :, lanes]], axis=0)
                value = block if value is None else jnp.where(chip == place, block, value)
            turned[pl.ds(col, 128, stride=COLS), pl.ds(0, 2 * ROWS)] = value.T
    for col in range(COLS - 1):
        lanes = pl.ds(128 * col, 128)

        def straight(turned, at):
            return turned[pl.ds(128 * at, 128), pl.ds(0, 2 * ROWS)]

        kept = jnp.where(core == 0, straight(even_turned, col), straight(odd_turned, col + 1)).T
        sent = jnp.where(core == 0, straight(odd_turned, col), straight(even_turned, col + 1)).T
        for plane in range(2):
            rows = slice(ROWS * plane, ROWS * (plane + 1))
            kept_out[plane, :, lanes] = kept[rows]
            sent_out[plane, :, lanes] = sent[rows]


def unwoven(pieces):
    whole = pl.BlockSpec(memory_space=pltpu.VMEM)
    half = jax.ShapeDtypeStruct((2, ROWS, LANES // 2), jnp.float32)
    return pl.pallas_call(
        unweave_kernel,
        out_shape=[half, half],
        in_specs=[whole] * len(pieces),
        out_specs=[whole, whole],
        scratch_shapes=[pltpu.VMEM((WINDOW, 128), jnp.float32)] * 2,
        compiler_params=pltpu.CompilerParams(vmem_limit_bytes=24 * 1024 * 1024),
    )(*pieces)


def squared(field):
    return field[0] * field[0] + field[1] * field[1]


def snake(turn):
    cons, tiles = lax.axis_size("con"), lax.axis_size("tile")
    pairs = []
    for con in range(cons):
        for tile in range(tiles):
            there = tile + (1 if con % 2 != turn else -1)
            other = (con, there) if 0 <= there < tiles else (con ^ 1, tile)
            pairs.append((con * tiles + tile, other[0] * tiles + other[1]))
    return pairs


def beside(value):
    return (
        lax.ppermute(value, BOTH, snake(0)),
        value,
        lax.ppermute(value, BOTH, snake(1)),
    )


def after(value, *others):
    return lax.optimization_barrier((value, *others))[0]


def body(first_guess, misfit, innovations, obs_cells, depth, base_speed, frequency):
    chips = lax.axis_size("con") // 2
    con = lax.axis_index("con")
    chip, core = con // 2, con % 2
    swap = [(i, i ^ 1) for i in range(2 * chips)]

    def window(value, side):
        return jnp.where(core == side, value[..., :WINDOW], value[..., -WINDOW:])

    def shared(value):
        mine, sent = window(value, 0), window(value, 1)
        got = lax.ppermute(sent, "con", swap)
        return jnp.where(core == 0, mine, got), jnp.where(core == 0, got, mine), sent

    field_even, field_odd, sent = shared(first_guess[0])
    raw_first, _, raw_last = beside(after(first_guess, sent)[0])
    square_odd = squared(field_odd)
    square_pair = squared(field_even) + square_odd
    later = window(base_speed, 0)
    for step in range(1, chips):
        pairs = [(i, i ^ (2 * step)) for i in range(2 * chips)]
        got = lax.ppermute(square_pair, "con", pairs)
        later = later + jnp.where(chip ^ step > chip, got, 0.0)
    start, later = woven([(later + square_odd, ROWS)], [(later, ROWS)])
    starts = beside(start)

    innovations = after(innovations, sent)
    lanes = jnp.arange(LANES, dtype=jnp.int32)
    rows = jnp.arange(ROWS, dtype=jnp.int32)
    at_lane = (obs_cells[:, None] % LANES == lanes[None]).astype(jnp.float32)
    at_row = (obs_cells[None] // LANES == rows[:, None]).astype(jnp.float32)
    added = jnp.dot(
        (innovations[0][:, None] * at_row[None]).reshape(2 * ROWS, -1),
        at_lane,
        precision=lax.Precision.HIGHEST,
        preferred_element_type=jnp.float32,
    )
    forcing = misfit[0].reshape(2 * ROWS, LANES) + added
    tones = jnp.broadcast_to(frequency, (8, LANES))
    force_even, force_odd, _ = shared(jnp.concatenate([forcing, tones]))
    tone_even, tone_odd = force_even[2 * ROWS :], force_odd[2 * ROWS :]
    flat = lambda field: field.reshape(2 * ROWS, WINDOW)
    forces, fields = woven(
        [(force_even, 2 * ROWS), (force_odd, 2 * ROWS), (window(depth, 0), ROWS)],
        [(flat(field_even), 2 * ROWS), (flat(field_odd), 2 * ROWS)],
    )
    forces = beside(forces)
    given = [window(value, 1) for value in (raw_first, raw_last)]
    got = lax.ppermute(
        jnp.where(core == 0, jnp.stack(given), jnp.stack(given[::-1])), "con", swap
    )
    sides = []
    for value, pair in ((raw_first, (got[0], got[1])), (raw_last, (got[1], got[0]))):
        mine = window(value, 0)
        sides.append(
            [
                (flat(jnp.where(core == 0, mine, pair[1])), 2 * ROWS),
                (flat(jnp.where(core == 0, pair[0], mine)), 2 * ROWS),
            ]
        )
    field_first, field_last = woven(*sides)
    fields = (field_first, fields, field_last)

    passed, results = None, []
    for now in range(chips):
        speeds = [starts]
        if now:
            up, down, passed = [
                lax.ppermute(passed, BOTH, hop_pairs(now - 1, shift)) for shift in (1, -1, 0)
            ]
            speeds.append([up, passed, down])
        solved, passed, speed = section(now, speeds, fields, forces, 0, tone_even, passed, later)
        results.append(solved)
        solved, passed = section(now, [beside(speed)], fields, forces, 2 * ROWS, tone_odd, passed)
        results.append(solved)

    kept, sent = unwoven(results)
    got = lax.ppermute(sent, "con", swap)
    result = jnp.where(
        core == 0,
        jnp.concatenate([kept, got], axis=-1),
        jnp.concatenate([got, kept], axis=-1),
    )
    return result[None]


def solution(mesh):
    placed = (
        P("con", None, "tile", None),
        P("con", None, "tile", None),
        P("con", None, "tile"),
        P("tile"),
        P("tile", None),
        P("tile", None),
        P("con"),
    )
    return jax.shard_map(
        body, mesh=mesh, in_specs=placed, out_specs=P("con", None, "tile", None), check_vma=False
    )
```

```python
import functools

import jax
import jax.numpy as jnp
from jax import lax
from jax.experimental import pallas as pl
from jax.experimental.pallas import tpu as pltpu
from jax.sharding import PartitionSpec as P

SWEEPS = 16
DRAG_COEF = 0.5
SHIFT_SIGMA = 0.1
ROWS = 16
LANES = 2048
WINDOW = 1152
COLS = WINDOW // 128
SPAN = 3 * ROWS
BOTH = ("con", "tile")


def hop_pairs(chip, shift):
    tiles = lax.axis_size("tile")
    return [
        (con * tiles + tile, (con + 2) * tiles + tile + step)
        for con, step in ((2 * chip, -shift), (2 * chip + 1, shift))
        for tile in range(tiles)
        if 0 <= tile + step < tiles
    ]


def sweep(source, target, gain, offset, base, blocks):
    for block in range(blocks):
        inside = pl.ds(base + 8 * block, 8)
        middle = pl.ds(8 + base + 8 * block, 8)
        above = pl.ds(7 + base + 8 * block, 8)
        below = pl.ds(9 + base + 8 * block, 8)
        cells = {
            (plane, col): source[plane, col, middle, :] for plane in range(2) for col in range(COLS)
        }
        for plane in range(2):
            cells[plane, -1] = pltpu.roll(cells[plane, COLS - 1], 1, 1)
            cells[plane, COLS] = pltpu.roll(cells[plane, 0], 127, 1)

        for col in range(COLS):
            total = []
            for plane in range(2):
                along = source[plane, col, above, :] + source[plane, col, below, :]
                across = cells[plane, col - 1] + cells[plane, col + 1]
                total.append(along + across)
            gain_real = gain[0, col, inside, :]
            gain_imag = gain[1, col, inside, :]
            target[0, col, middle, :] = offset[0, col, inside, :] + (
                gain_real * total[0] - gain_imag * total[1]
            )
            target[1, col, middle, :] = offset[1, col, inside, :] + (
                gain_real * total[1] + gain_imag * total[0]
            )


def section_kernel(chip, speeds, carried, more, first, *refs):
    refs = list(refs)
    take = lambda count: [refs.pop(0) for _ in range(count)]
    speed_refs = [take(3) for _ in range(speeds)]
    field_refs, force_refs = take(3), take(3)
    (tone_ref,) = take(1)
    passed_ref = take(1)[0] if carried else None
    later_ref = take(1)[0] if more else None
    adjoint_out, passed_out = take(2)
    speed_out = take(1)[0] if more else None
    gain, offset, here, there = refs
    con = lax.axis_index("con")
    tile = lax.axis_index("tile")
    tiles = lax.axis_size("tile")
    core = con % 2

    @pl.when(con // 2 == chip)
    def _():
        lane2 = lax.broadcasted_iota(jnp.int32, (ROWS, 128), 1)
        nothing = jnp.zeros((8, 128), jnp.float32)
        angular = jnp.broadcast_to(tone_ref[0:1, 0:128], (ROWS, 128))
        first_row = pl.multiple_of(2 * ROWS * (1 - core), ROWS)
        places = (first_row, ROWS, pl.multiple_of(2 * ROWS - first_row, ROWS))
        above, below = tile > 0, tile < tiles - 1
        inner = [
            jnp.logical_or(
                jnp.logical_and(core != turn, above), jnp.logical_and(core == turn, below)
            )
            for turn in range(2)
        ]
        for col in range(COLS):
            lanes = pl.ds(128 * col, 128)
            for buffer in (here, there):
                for plane in range(2):
                    buffer[plane, col, pl.ds(0, 8), :] = nothing
                    buffer[plane, col, pl.ds(8 + SPAN, 8), :] = nothing
            for piece in range(3):
                speed_sq = speed_refs[0][piece][:, lanes]
                if speeds == 2:
                    speed_sq = speed_sq + speed_refs[1][piece][:, lanes]
                deep = force_refs[piece][pl.ds(4 * ROWS, ROWS), lanes]
                drag = DRAG_COEF * jnp.sqrt(speed_sq)
                scaled = deep / (drag * drag + angular * angular)
                gain_real = scaled * drag
                gain_imag = scaled * angular
                diag_real = SHIFT_SIGMA + 4.0 * gain_real
                diag_imag = angular + 4.0 * gain_imag
                inverse = 1.0 / (diag_real * diag_real + diag_imag * diag_imag)
                inv_real = diag_real * inverse
                inv_imag = -diag_imag * inverse
                field_real, field_imag, force_real, force_imag = (
                    part[piece][pl.ds(first + ROWS * plane, ROWS), lanes]
                    for part in (field_refs, force_refs)
                    for plane in range(2)
                )
                values = [
                    gain_real * inv_real - gain_imag * inv_imag,
                    gain_real * inv_imag + gain_imag * inv_real,
                    force_real * inv_real - force_imag * inv_imag,
                    force_real * inv_imag + force_imag * inv_real,
                    field_real,
                    field_imag,
                ]
                keep = None
                if piece != 1:
                    keep = jnp.broadcast_to(inner[piece // 2], (ROWS, 128))
                edge = None
                if col == 0:
                    edge = (lane2 != 0) | (core == 0)
                if col == COLS - 1:
                    edge = (lane2 != 127) | (core == 1)
                if edge is not None:
                    keep = edge if keep is None else keep & edge
                if keep is not None:
                    values = [jnp.where(keep, value, 0.0) for value in values]
                inside = pl.ds(places[piece], ROWS)
                shifted = pl.ds(8 + places[piece], ROWS)
                gain[0, col, inside, :] = values[0]
                gain[1, col, inside, :] = values[1]
                offset[0, col, inside, :] = values[2]
                offset[1, col, inside, :] = values[3]
                here[0, col, shifted, :] = values[4]
                here[1, col, shifted, :] = values[5]

        for phase in range(4):

            def step(_, carry):
                sweep(here, there, gain, offset, 4 * phase, 6 - phase)
                sweep(there, here, gain, offset, 4 * phase, 6 - phase)
                return carry

            lax.fori_loop(0, SWEEPS // 8, step, 0)
        for col in range(COLS):
            lanes = pl.ds(128 * col, 128)
            real = here[0, col, pl.ds(8 + ROWS, ROWS), :]
            imag = here[1, col, pl.ds(8 + ROWS, ROWS), :]
            adjoint_out[0, :, lanes] = real
            adjoint_out[1, :, lanes] = imag
            total = real * real + imag * imag
            if carried:
                total = total + passed_ref[:, lanes]
            passed_out[:, lanes] = total
            if more:
                speed_out[:, lanes] = total + later_ref[:, lanes]


def section(chip, speeds, fields, forces, first, tone, passed=None, later=None):
    tile_shape = jax.ShapeDtypeStruct((ROWS, WINDOW), jnp.float32)
    pair_shape = jax.ShapeDtypeStruct((2, ROWS, WINDOW), jnp.float32)
    operands = [piece for term in speeds for piece in term] + [*fields, *forces, tone]
    operands += [value for value in (passed, later) if value is not None]
    outs = [pair_shape, tile_shape] + ([tile_shape] if later is not None else [])
    whole = pl.BlockSpec(memory_space=pltpu.VMEM)
    vmem = lambda rows: pltpu.VMEM((2, COLS, rows, 128), jnp.float32)
    return pl.pallas_call(
        functools.partial(
            section_kernel, chip, len(speeds), passed is not None, later is not None, first
        ),
        out_shape=outs,
        in_specs=[whole] * len(operands),
        out_specs=[whole] * len(outs),
        scratch_shapes=[vmem(SPAN), vmem(SPAN), vmem(SPAN + 16), vmem(SPAN + 16)],
        compiler_params=pltpu.CompilerParams(vmem_limit_bytes=24 * 1024 * 1024),
    )(*operands)


def weave(blocks, store, turned):
    rows = blocks[0].shape[0]
    for col in range(COLS):
        turned[pl.ds(128 * col, 128), pl.ds(0, rows)] = blocks[col].T
    for col in range(COLS):
        store(col, turned[pl.ds(col, 128, stride=COLS), pl.ds(0, rows)].T)


def weave_kernel(groups, *refs):
    refs = list(refs)
    turned = refs.pop()
    outs = refs[-len(groups) :]
    for group, out in zip(groups, outs):
        parts = [(refs.pop(0), rows) for rows in group]
        blocks = [
            jnp.concatenate(
                [part[pl.ds(0, rows), pl.ds(128 * col, 128)] for part, rows in parts], axis=0
            )
            for col in range(COLS)
        ]

        def store(col, value):
            out[:, pl.ds(128 * col, 128)] = value

        weave(blocks, store, turned)


def woven(*groups):
    whole = pl.BlockSpec(memory_space=pltpu.VMEM)
    sizes = [[rows for _, rows in group] for group in groups]
    operands = [value for group in groups for value, _ in group]
    return pl.pallas_call(
        functools.partial(weave_kernel, sizes),
        out_shape=[jax.ShapeDtypeStruct((sum(rows), WINDOW), jnp.float32) for rows in sizes],
        in_specs=[whole] * len(operands),
        out_specs=[whole] * len(groups),
        scratch_shapes=[pltpu.VMEM((WINDOW, 128), jnp.float32)],
        compiler_params=pltpu.CompilerParams(vmem_limit_bytes=24 * 1024 * 1024),
    )(*operands)


def unweave_kernel(*refs):
    refs = list(refs)
    kept_out, sent_out, even_turned, odd_turned = refs[-4:]
    evens, odds = refs[:-4][0::2], refs[:-4][1::2]
    con = lax.axis_index("con")
    chip, core = con // 2, con % 2
    for pieces, turned in ((evens, even_turned), (odds, odd_turned)):
        for col in range(COLS):
            lanes = pl.ds(128 * col, 128)
            value = None
            for place, piece in enumerate(pieces):
                block = jnp.concatenate([piece[0, :, lanes], piece[1, :, lanes]], axis=0)
                value = block if value is None else jnp.where(chip == place, block, value)
            turned[pl.ds(col, 128, stride=COLS), pl.ds(0, 2 * ROWS)] = value.T
    for col in range(COLS - 1):
        lanes = pl.ds(128 * col, 128)

        def straight(turned, at):
            return turned[pl.ds(128 * at, 128), pl.ds(0, 2 * ROWS)]

        kept = jnp.where(core == 0, straight(even_turned, col), straight(odd_turned, col + 1)).T
        sent = jnp.where(core == 0, straight(odd_turned, col), straight(even_turned, col + 1)).T
        for plane in range(2):
            rows = slice(ROWS * plane, ROWS * (plane + 1))
            kept_out[plane, :, lanes] = kept[rows]
            sent_out[plane, :, lanes] = sent[rows]


def unwoven(pieces):
    whole = pl.BlockSpec(memory_space=pltpu.VMEM)
    half = jax.ShapeDtypeStruct((2, ROWS, LANES // 2), jnp.float32)
    return pl.pallas_call(
        unweave_kernel,
        out_shape=[half, half],
        in_specs=[whole] * len(pieces),
        out_specs=[whole, whole],
        scratch_shapes=[pltpu.VMEM((WINDOW, 128), jnp.float32)] * 2,
        compiler_params=pltpu.CompilerParams(vmem_limit_bytes=24 * 1024 * 1024),
    )(*pieces)


def squared(field):
    return field[0] * field[0] + field[1] * field[1]


def snake(turn):
    cons, tiles = lax.axis_size("con"), lax.axis_size("tile")
    pairs = []
    for con in range(cons):
        for tile in range(tiles):
            there = tile + (1 if con % 2 != turn else -1)
            other = (con, there) if 0 <= there < tiles else (con ^ 1, tile)
            pairs.append((con * tiles + tile, other[0] * tiles + other[1]))
    return pairs


def beside(value):
    return (
        lax.ppermute(value, BOTH, snake(0)),
        value,
        lax.ppermute(value, BOTH, snake(1)),
    )


def after(value, *others):
    return lax.optimization_barrier((value, *others))[0]


def body(first_guess, misfit, innovations, obs_cells, depth, base_speed, frequency):
    chips = lax.axis_size("con") // 2
    con = lax.axis_index("con")
    chip, core = con // 2, con % 2
    swap = [(i, i ^ 1) for i in range(2 * chips)]

    def window(value, side):
        return jnp.where(core == side, value[..., :WINDOW], value[..., -WINDOW:])

    def shared(value):
        mine, sent = window(value, 0), window(value, 1)
        got = lax.ppermute(sent, "con", swap)
        return jnp.where(core == 0, mine, got), jnp.where(core == 0, got, mine), sent

    field_even, field_odd, sent = shared(first_guess[0])
    raw_first, _, raw_last = beside(after(first_guess, sent)[0])
    square_odd = squared(field_odd)
    square_pair = squared(field_even) + square_odd
    later = window(base_speed, 0)
    for step in range(1, chips):
        pairs = [(i, i ^ (2 * step)) for i in range(2 * chips)]
        got = lax.ppermute(square_pair, "con", pairs)
        later = later + jnp.where(chip ^ step > chip, got, 0.0)
    (start,) = woven([(later + square_odd, ROWS)])
    starts = beside(start)

    innovations = after(innovations, sent)
    lanes = jnp.arange(LANES, dtype=jnp.int32)
    rows = jnp.arange(ROWS, dtype=jnp.int32)
    at_lane = (obs_cells[:, None] % LANES == lanes[None]).astype(jnp.float32)
    at_row = (obs_cells[None] // LANES == rows[:, None]).astype(jnp.float32)
    added = jnp.dot(
        (innovations[0][:, None] * at_row[None]).reshape(2 * ROWS, -1),
        at_lane,
        precision=lax.Precision.HIGHEST,
        preferred_element_type=jnp.float32,
    )
    forcing = misfit[0].reshape(2 * ROWS, LANES) + added
    tones = jnp.broadcast_to(frequency, (8, LANES))
    force_even, force_odd, _ = shared(jnp.concatenate([forcing, tones]))
    tone_even, tone_odd = force_even[2 * ROWS :], force_odd[2 * ROWS :]
    flat = lambda field: field.reshape(2 * ROWS, WINDOW)
    forces, fields = woven(
        [(force_even, 2 * ROWS), (force_odd, 2 * ROWS), (window(depth, 0), ROWS)],
        [(flat(field_even), 2 * ROWS), (flat(field_odd), 2 * ROWS)],
    )
    forces = beside(forces)
    given = [window(value, 1) for value in (raw_first, raw_last)]
    got = lax.ppermute(
        jnp.where(core == 0, jnp.stack(given), jnp.stack(given[::-1])), "con", swap
    )
    sides = []
    for value, pair in ((raw_first, (got[0], got[1])), (raw_last, (got[1], got[0]))):
        mine = window(value, 0)
        sides.append(
            [
                (flat(jnp.where(core == 0, mine, pair[1])), 2 * ROWS),
                (flat(jnp.where(core == 0, pair[0], mine)), 2 * ROWS),
            ]
        )
    field_first, field_last, later = woven(*sides, [(later, ROWS)])
    fields = (field_first, fields, field_last)

    passed, results = None, []
    for now in range(chips):
        speeds = [starts]
        if now:
            up, down, passed = [
                lax.ppermute(passed, BOTH, hop_pairs(now - 1, shift)) for shift in (1, -1, 0)
            ]
            speeds.append([up, passed, down])
        solved, passed, speed = section(now, speeds, fields, forces, 0, tone_even, passed, later)
        results.append(solved)
        solved, passed = section(now, [beside(speed)], fields, forces, 2 * ROWS, tone_odd, passed)
        results.append(solved)

    kept, sent = unwoven(results)
    got = lax.ppermute(sent, "con", swap)
    result = jnp.where(
        core == 0,
        jnp.concatenate([kept, got], axis=-1),
        jnp.concatenate([got, kept], axis=-1),
    )
    return result[None]


def solution(mesh):
    placed = (
        P("con", None, "tile", None),
        P("con", None, "tile", None),
        P("con", None, "tile"),
        P("tile"),
        P("tile", None),
        P("tile", None),
        P("con"),
    )
    return jax.shard_map(
        body, mesh=mesh, in_specs=placed, out_specs=P("con", None, "tile", None), check_vma=False
    )
```
